256 devices in a mesh: row: 16 (over z, core), col: 16 (over y, x).
Axes of the slice: x: 4, y: 4, z: 8, core: 2. Of those that a mesh axis runs over, the one named last changes fastest.
Arguments:
- matrix: float32 [196608, 2048], P('row', 'col')
- plan: int32 [16], replicated, may hold values from 0 to 1
Outputs:
- rotated_matrix: float32 [196608, 2048], P('row', 'col')
The draws below stay inside these ranges and needn't reach their ends.
Inputs may be any that keep to these rules, and one draw needn't show every extreme that they name: `plan`: entry p picks block 2p (0) or block 2p+1 (1) of pair p.
All inputs are finite; a program needn't handle non-finite values.
Results may differ from the reference program's by a relative error of at most 0.0003.
Values sent between devices are 32-bit elements; how exact they have to be, the bound alone decides.
No kernel may reach another device: no remote copies, remote signals or barrier semaphores. Data moves between devices by JAX's collectives and lax.ppermute only.
A program may use at most 128 MiB of HBM per device.

```python
import jax
import jax.numpy as jnp
from jax import lax

BLK = 64
ITERS = 3
ROWS = 196608
PAIRS = 16
COLS = 2048


def draw_matrix(key, part):
    key = jax.random.fold_in(key, 11)
    subkeys = jax.random.split(key, 4)
    common = jax.random.normal(subkeys[3], (ROWS, 1), jnp.float32)
    noise_part = jax.random.normal(subkeys[0], (ROWS, COLS), jnp.float32)
    scales = jnp.exp(jax.random.uniform(subkeys[1], (COLS,), jnp.float32, jnp.log(0.6), jnp.log(1.6)))
    mixing = jax.random.uniform(subkeys[2], (COLS,), jnp.float32, -0.25, 0.25)
    values = scales[None, :] * (noise_part + mixing[None, :] * common)
    return values.astype(jnp.float32)


def with_ends(array, stream_key, low, high):
    extent = array.shape
    spot = [jax.random.randint(jax.random.fold_in(stream_key, axis), (), 0, extent[axis]) for axis in range(len(extent))]
    array = array.at[tuple(spot)].set(low)
    longest = extent.index(max(extent))
    spot[longest] = (spot[longest] + 1) % extent[longest]
    return array.at[tuple(spot)].set(high)


def setup_inputs(seed: int = 0) -> dict:
    arg_keys = jax.random.split(jax.random.key(seed), 3)
    matrix = draw_matrix(jax.random.fold_in(arg_keys[2], 71), 0)
    plan = with_ends(jax.random.randint(arg_keys[1], (PAIRS,), 0, 2), jax.random.fold_in(arg_keys[1], 1), 0, 1).astype(jnp.int32)
    return {"matrix": matrix, "plan": plan}


def rotation(gram_matrix):
    order = gram_matrix.shape[0]
    basis = jnp.eye(order, dtype=jnp.float32)
    for step_index in range(ITERS):
        product = jnp.dot(gram_matrix.astype(jnp.float32), basis.astype(jnp.float32), precision=lax.Precision.HIGHEST, preferred_element_type=jnp.float32)
        normal_eq = jnp.dot(product.T.astype(jnp.float32), product.astype(jnp.float32), precision=lax.Precision.HIGHEST, preferred_element_type=jnp.float32)
        factor = jnp.linalg.cholesky(normal_eq)
        basis = lax.linalg.triangular_solve(factor, product, left_side=False, lower=True, transpose_a=True)
    return basis

def gram_of(columns):
    return jnp.dot(columns.T.astype(jnp.float32), columns.astype(jnp.float32), precision=lax.Precision.HIGHEST, preferred_element_type=jnp.float32)

def turn_pair(columns):
    return jnp.dot(columns.astype(jnp.float32), rotation(gram_of(columns)).astype(jnp.float32), precision=lax.Precision.HIGHEST, preferred_element_type=jnp.float32)

def reference(matrix, plan):
    stacked = jnp.moveaxis(matrix.reshape(ROWS, PAIRS, 2 * BLK), 1, 0)
    turned = lax.map(turn_pair, stacked)
    front_half = turned[:, :, :BLK]
    back_half = turned[:, :, BLK:]
    leaver = (plan == 1)[:, None, None]
    leaving = jnp.where(leaver, back_half, front_half)
    staying = jnp.where(leaver, front_half, back_half)
    arrived = jnp.roll(leaving, 1, axis=0)
    rotated = lax.map(turn_pair, jnp.concatenate([staying, arrived], axis=2))
    new_stay = rotated[:, :, :BLK]
    new_leave = jnp.roll(rotated[:, :, BLK:], -1, axis=0)
    blocks = jnp.where(leaver, jnp.concatenate([new_stay, new_leave], axis=2), jnp.concatenate([new_leave, new_stay], axis=2))
    return jnp.moveaxis(blocks, 0, 1).reshape(ROWS, COLS)
```

```python
import functools

import jax
import jax.numpy as jnp
from jax import lax
from jax.experimental import pallas as pl
from jax.experimental.pallas import tpu as pltpu
from jax.sharding import PartitionSpec as P

ITERS = 3
ORDER = 128
HALF = 64
GROUP = 8
GRAM_ROWS = 1024
TURN_ROWS = 1024
F32 = jnp.float32
BF16 = jnp.bfloat16


def split_two(value):
    high = value.astype(BF16)
    low = (value - high.astype(F32)).astype(BF16)
    return high, low


def split_three(value):
    high = value.astype(BF16)
    rest = value - high.astype(F32)
    middle = rest.astype(BF16)
    low = (rest - middle.astype(F32)).astype(BF16)
    return high, middle, low


def dot_bf16(left, right, dims):
    return lax.dot_general(left, right, (dims, ((), ())), preferred_element_type=F32)


def dot_six(left, right, transpose_right):
    lh, lm, ll = split_three(left)
    rh, rm, rl = split_three(right)
    axis = 1 if transpose_right else 0
    dims = ((1,), (axis,))
    total = None
    for (la, ra), (lb, rb) in (((lh, rl), (ll, rh)), ((lm, rm), (lm, rh)), ((lh, rm), (lh, rh))):
        term = dot_bf16(
            jnp.concatenate([la, lb], axis=1), jnp.concatenate([ra, rb], axis=axis), dims
        )
        total = term if total is None else total + term
    return total


def across(column, rows):
    return jnp.broadcast_to(column, (rows, ORDER))


def orthonormal_rows(normal, rows_in):
    done = []
    spot = lax.broadcasted_iota(jnp.int32, (GROUP, ORDER), 0)
    for start in range(0, ORDER, GROUP):
        tail = ORDER - start - GROUP
        head_n, head_y = normal[:GROUP], rows_in[:GROUP]
        tail_n, tail_y = normal[GROUP:], rows_in[GROUP:]
        head_c = [across(head_n[:, start + j : start + j + 1], GROUP) for j in range(GROUP)]
        tail_c = [across(tail_n[:, start + j : start + j + 1], tail) for j in range(GROUP)] if tail else []
        pivots = head_c[0]
        for k in range(GROUP):
            pivot = across(head_c[k][k : k + 1], GROUP)
            inverse = 1.0 / pivot
            row_n = head_n[k : k + 1]
            row_y = head_y[k : k + 1]
            if k:
                pivots = jnp.where(spot >= k, pivot, pivots)
            else:
                pivots = pivot
            cross = [head_c[j][k : k + 1] for j in range(k + 1, GROUP)]
            if k < GROUP - 1:
                scaled = jnp.where(spot > k, head_c[k] * inverse, 0.0)
                head_n = head_n - scaled * row_n
                head_y = head_y - scaled * row_y
                for j in range(k + 1, GROUP):
                    head_c[j] = head_c[j] - scaled * cross[j - k - 1]
            if tail:
                scaled = tail_c[k] * inverse[:1]
                tail_n = tail_n - scaled * row_n
                tail_y = tail_y - scaled * row_y
                for j in range(k + 1, GROUP):
                    tail_c[j] = tail_c[j] - scaled * cross[j - k - 1]
        done.append(head_y * lax.rsqrt(pivots))
        normal, rows_in = tail_n, tail_y
    return jnp.concatenate(done, axis=0)


def rotation_kernel(gram_ref, out_ref):
    gram = gram_ref[...]
    gram = gram * (1.0 / jnp.max(jnp.abs(gram)))

    def turn(rows):
        out_ref[...] = orthonormal_rows(dot_six(rows, rows, True), rows)

    turn(gram)

    def step(_, carry):
        turn(dot_six(out_ref[...], gram, False))
        return carry

    lax.fori_loop(1, ITERS, step, 0)


def rotation_rows(gram_total):
    return pl.pallas_call(
        rotation_kernel,
        out_shape=jax.ShapeDtypeStruct((ORDER, ORDER), F32),
        in_specs=[pl.BlockSpec(memory_space=pltpu.VMEM)],
        out_specs=pl.BlockSpec(memory_space=pltpu.VMEM),
        compiler_params=pltpu.CompilerParams(vmem_limit_bytes=32 * 2**20),
        name="rotation",
    )(gram_total)


def gram_kernel(x_ref, out_ref, total):
    step = pl.program_id(0)

    @pl.when(step == 0)
    def _():
        total[...] = jnp.zeros_like(total)

    high, low = split_two(x_ref[...])
    both = jnp.concatenate([high, low], axis=1)
    total[...] += dot_bf16(high, both, ((0,), (0,)))

    @pl.when(step == pl.num_programs(0) - 1)
    def _():
        mixed = total[:, ORDER:]
        out_ref[...] = total[:, :ORDER] + (mixed + mixed.T)


def gram_of(columns):
    rows = columns.shape[0]
    return pl.pallas_call(
        gram_kernel,
        grid=(rows // GRAM_ROWS,),
        out_shape=jax.ShapeDtypeStruct((ORDER, ORDER), F32),
        in_specs=[pl.BlockSpec((GRAM_ROWS, ORDER), lambda i: (i, 0))],
        out_specs=pl.BlockSpec((ORDER, ORDER), lambda i: (0, 0)),
        scratch_shapes=[pltpu.VMEM((ORDER, 2 * ORDER), F32)],
        compiler_params=pltpu.CompilerParams(vmem_limit_bytes=32 * 2**20),
        name="gram",
    )(columns)


def turn_kernel(flag_ref, rows_ref, top_ref, bottom_ref, early_ref, late_ref, high, low):
    @pl.when(pl.program_id(0) == 0)
    def _():
        front, back = rows_ref[:HALF], rows_ref[HALF:]
        is_back = flag_ref[0] == 1
        early = jnp.where(is_back, back, front)
        late = jnp.where(is_back, front, back)
        none = jnp.zeros_like(early)
        weights = jnp.concatenate(
            [
                jnp.concatenate([early, none, late, none], axis=0),
                jnp.concatenate([none, early, none, late], axis=0),
            ],
            axis=1,
        ).T
        high[...], low[...] = split_two(weights)

    xh, xl = split_two(jnp.concatenate([top_ref[...], bottom_ref[...]], axis=1))
    dims = ((1,), (0,))
    out = dot_bf16(xh, high[...], dims) + (dot_bf16(xh, low[...], dims) + dot_bf16(xl, high[...], dims))
    early_ref[...] = out[:, :ORDER]
    late_ref[...] = out[:, ORDER:]


def turn(columns, turn_rows, early_is_back):
    rows = columns.shape[0] // 2
    steps = rows // TURN_ROWS
    packed = jax.ShapeDtypeStruct((rows, ORDER), F32)
    block = (TURN_ROWS, ORDER)
    return pl.pallas_call(
        turn_kernel,
        grid=(steps,),
        out_shape=(packed, packed),
        in_specs=[
            pl.BlockSpec(memory_space=pltpu.SMEM),
            pl.BlockSpec((ORDER, ORDER), lambda i: (0, 0)),
            pl.BlockSpec(block, lambda i: (i, 0)),
            pl.BlockSpec(block, lambda i: (i + steps, 0)),
        ],
        out_specs=(pl.BlockSpec(block, lambda i: (i, 0)), pl.BlockSpec(block, lambda i: (i, 0))),
        scratch_shapes=[pltpu.VMEM((2 * ORDER, 2 * ORDER), BF16)] * 2,
        compiler_params=pltpu.CompilerParams(vmem_limit_bytes=32 * 2**20),
        name="turn",
    )(early_is_back, turn_rows, columns, columns)


def half_roll(value, axis):
    return pltpu.roll(value, HALF, axis)


def low_lanes(shape):
    return lax.broadcasted_iota(jnp.int32, shape, 1) < HALF


def pair_gram_kernel(core_ref, own_ref, come_ref, out_ref, total):
    step = pl.program_id(0)

    @pl.when(step == 0)
    def _():
        total[...] = jnp.zeros_like(total)

    high, low = split_two(jnp.concatenate([own_ref[...], come_ref[...]], axis=1))
    total[...] += dot_bf16(high, jnp.concatenate([high, low], axis=1), ((0,), (0,)))

    @pl.when(step == pl.num_programs(0) - 1)
    def _():
        mixed = total[:, 2 * ORDER :]
        whole = total[:, : 2 * ORDER] + (mixed + mixed.T)
        tops = jnp.concatenate([whole[:HALF], whole[ORDER : ORDER + HALF]], axis=0)
        bottoms = jnp.concatenate([whole[HALF:ORDER], whole[ORDER + HALF :]], axis=0)
        first = low_lanes((ORDER, ORDER))
        gram = jnp.where(first, tops[:, :ORDER], half_roll(tops[:, ORDER:], 1)) + jnp.where(
            first, half_roll(bottoms[:, :ORDER], 1), bottoms[:, ORDER:]
        )
        swapped = half_roll(half_roll(gram, 1), 0)
        out_ref[...] = jnp.where(core_ref[0] == 1, swapped, gram)


def pair_gram(core, own, come):
    rows = own.shape[0]
    block = pl.BlockSpec((GRAM_ROWS, ORDER), lambda i: (i, 0))
    return pl.pallas_call(
        pair_gram_kernel,
        grid=(rows // GRAM_ROWS,),
        out_shape=jax.ShapeDtypeStruct((ORDER, ORDER), F32),
        in_specs=[pl.BlockSpec(memory_space=pltpu.SMEM), block, block],
        out_specs=pl.BlockSpec((ORDER, ORDER), lambda i: (0, 0)),
        scratch_shapes=[pltpu.VMEM((2 * ORDER, 4 * ORDER), F32)],
        compiler_params=pltpu.CompilerParams(vmem_limit_bytes=32 * 2**20),
        name="pair_gram",
    )(core, own, come)


def finish_kernel(
    flags_ref, mine_ref, other_ref, early_ref, late_ref, come_ref, last_ref, out_ref, high, low
):
    @pl.when(pl.program_id(0) == 0)
    def _():
        swap = flags_ref[1] == 1

        def ordered(rows):
            return jnp.where(swap, half_roll(half_roll(rows, 1), 0), rows)

        first = low_lanes((HALF, ORDER))
        none = jnp.zeros((HALF, ORDER), F32)
        late_rows = ordered(mine_ref[...])[:HALF]
        early_rows = ordered(other_ref[...])[HALF:]
        late_own, late_come = jnp.where(first, late_rows, 0.0), jnp.where(first, 0.0, late_rows)
        early_last, early_own = jnp.where(first, early_rows, 0.0), jnp.where(first, 0.0, early_rows)

        def lanes(parts):
            return jnp.concatenate(parts, axis=1)

        early_top = lanes([half_roll(early_own, 1), none, none, early_last])
        early_bottom = lanes([early_own, none, none, half_roll(early_last, 1)])
        late_top = lanes([none, late_own, half_roll(late_come, 1), none])
        late_bottom = lanes([none, half_roll(late_own, 1), late_come, none])
        is_back = flags_ref[0] == 1
        weights = jnp.concatenate(
            [
                jnp.where(is_back, late_top, early_top),
                jnp.where(is_back, early_top, late_top),
                jnp.where(is_back, late_bottom, early_bottom),
                jnp.where(is_back, early_bottom, late_bottom),
            ],
            axis=0,
        ).T
        high[...], low[...] = split_two(weights)

    joined = jnp.concatenate([early_ref[...], late_ref[...], come_ref[...], last_ref[...]], axis=1)
    xh, xl = split_two(joined)
    dims = ((1,), (0,))
    out = dot_bf16(xh, high[...], dims) + (dot_bf16(xh, low[...], dims) + dot_bf16(xl, high[...], dims))
    out_ref[0] = out[:, :ORDER]
    out_ref[1] = out[:, ORDER:]


def finish(flags, mine, other, early, late, come, last):
    rows = early.shape[0]
    square = pl.BlockSpec((ORDER, ORDER), lambda i: (0, 0))
    block = pl.BlockSpec((TURN_ROWS, ORDER), lambda i: (i, 0))
    out = pl.pallas_call(
        finish_kernel,
        grid=(rows // TURN_ROWS,),
        out_shape=jax.ShapeDtypeStruct((2, rows, ORDER), F32),
        in_specs=[pl.BlockSpec(memory_space=pltpu.SMEM), square, square, block, block, block, block],
        out_specs=pl.BlockSpec((2, TURN_ROWS, ORDER), lambda i: (0, i, 0)),
        scratch_shapes=[pltpu.VMEM((4 * ORDER, 2 * ORDER), BF16)] * 2,
        compiler_params=pltpu.CompilerParams(vmem_limit_bytes=32 * 2**20),
        name="finish",
    )(flags, mine, other, early, late, come, last)
    return out.reshape(2 * rows, ORDER)


def moved(array, target):
    rows, cols = lax.axis_size("row"), lax.axis_size("col")
    pairs = []
    for row in range(rows):
        for col in range(cols):
            to_row, to_col = target(row, col)
            pairs.append((row * cols + col, (to_row % rows) * cols + to_col % cols))
    return lax.ppermute(array, ("row", "col"), pairs)


def outward(row, col):
    return row, col + (1 if row % 2 == 0 else -1)


def inward(row, col):
    return row, col + (-1 if row % 2 == 0 else 1)


def swap_rows(by):
    return lambda row, col: (row ^ by, col)


def partner(row, col):
    return (row + 1, col - 1) if row % 2 == 0 else (row - 1, col + 1)


def local(matrix, plan):
    core = lax.axis_index("row") % 2
    leaver = plan[lax.axis_index("col")]
    early_is_back = leaver ^ core
    gram = gram_of(matrix)
    for by in (1, 2, 4, 8):
        gram = gram + moved(gram, swap_rows(by))
    early, late = turn(matrix, rotation_rows(gram), early_is_back.reshape(1))
    come = moved(early, outward)
    late, come = lax.optimization_barrier((late, come))
    last = moved(late, inward)
    second = pair_gram(core.reshape(1), late, come)
    second = second + moved(second, partner)
    for by in (2, 4, 8):
        second = second + moved(second, swap_rows(by))
    mine = rotation_rows(second)
    other = moved(mine, swap_rows(1))
    return finish(jnp.stack([early_is_back, core]), mine, other, early, late, come, last)


def solution(mesh):
    in_specs = (P("row", "col"), P())
    out_specs = P("row", "col")
    return jax.shard_map(local, mesh=mesh, in_specs=in_specs, out_specs=out_specs, check_vma=False)
```

```python
import functools

import jax
import jax.numpy as jnp
from jax import lax
from jax.experimental import pallas as pl
from jax.experimental.pallas import tpu as pltpu
from jax.sharding import PartitionSpec as P

ITERS = 3
ORDER = 128
HALF = 64
GROUP = 8
TILE = 512
RAW_TILES = 6
GRAM_LIMIT = 48
F32 = jnp.float32
BF16 = jnp.bfloat16


def split_two(value):
    high = value.astype(BF16)
    low = (value - high.astype(F32)).astype(BF16)
    return high, low


def split_three(value):
    high = value.astype(BF16)
    rest = value - high.astype(F32)
    middle = rest.astype(BF16)
    low = (rest - middle.astype(F32)).astype(BF16)
    return high, middle, low


def dot_bf16(left, right, dims):
    return lax.dot_general(left, right, (dims, ((), ())), preferred_element_type=F32)


def dot_six(left, right, transpose_right):
    lh, lm, ll = split_three(left)
    rh, rm, rl = split_three(right)
    axis = 1 if transpose_right else 0
    dims = ((1,), (axis,))
    total = None
    for (la, ra), (lb, rb) in (((lh, rl), (ll, rh)), ((lm, rm), (lm, rh)), ((lh, rm), (lh, rh))):
        term = dot_bf16(
            jnp.concatenate([la, lb], axis=1), jnp.concatenate([ra, rb], axis=axis), dims
        )
        total = term if total is None else total + term
    return total


def across(column, rows):
    return jnp.broadcast_to(column, (rows, ORDER))


def orthonormal_rows(normal, rows_in):
    done = []
    spot = lax.broadcasted_iota(jnp.int32, (GROUP, ORDER), 0)
    for start in range(0, ORDER, GROUP):
        tail = ORDER - start - GROUP
        head_n, head_y = normal[:GROUP], rows_in[:GROUP]
        tail_n, tail_y = normal[GROUP:], rows_in[GROUP:]
        head_c = [across(head_n[:, start + j : start + j + 1], GROUP) for j in range(GROUP)]
        tail_c = [across(tail_n[:, start + j : start + j + 1], tail) for j in range(GROUP)] if tail else []
        pivots = head_c[0]
        for k in range(GROUP):
            pivot = across(head_c[k][k : k + 1], GROUP)
            inverse = 1.0 / pivot
            row_n = head_n[k : k + 1]
            row_y = head_y[k : k + 1]
            if k:
                pivots = jnp.where(spot >= k, pivot, pivots)
            else:
                pivots = pivot
            cross = [head_c[j][k : k + 1] for j in range(k + 1, GROUP)]
            if k < GROUP - 1:
                scaled = jnp.where(spot > k, head_c[k] * inverse, 0.0)
                head_n = head_n - scaled * row_n
                head_y = head_y - scaled * row_y
                for j in range(k + 1, GROUP):
                    head_c[j] = head_c[j] - scaled * cross[j - k - 1]
            if tail:
                scaled = tail_c[k] * inverse[:1]
                tail_n = tail_n - scaled * row_n
                tail_y = tail_y - scaled * row_y
                for j in range(k + 1, GROUP):
                    tail_c[j] = tail_c[j] - scaled * cross[j - k - 1]
        done.append(head_y * lax.rsqrt(pivots))
        normal, rows_in = tail_n, tail_y
    return jnp.concatenate(done, axis=0)


def rotation_kernel(flag_ref, gram_ref, out_ref, half_ref):
    gram = gram_ref[...]
    gram = gram * (1.0 / jnp.max(jnp.abs(gram)))

    def turn(rows):
        out_ref[...] = orthonormal_rows(dot_six(rows, rows, True), rows)

    turn(gram)

    def step(_, carry):
        turn(dot_six(out_ref[...], gram, False))
        return carry

    lax.fori_loop(1, ITERS, step, 0)
    half_ref[...] = jnp.where(flag_ref[0] == 1, out_ref[:HALF], out_ref[HALF:])


def rotation_rows(flag, gram_total):
    vmem = pl.BlockSpec(memory_space=pltpu.VMEM)
    return pl.pallas_call(
        rotation_kernel,
        out_shape=(
            jax.ShapeDtypeStruct((ORDER, ORDER), F32),
            jax.ShapeDtypeStruct((HALF, ORDER), F32),
        ),
        in_specs=[pl.BlockSpec(memory_space=pltpu.SMEM), vmem],
        out_specs=(vmem, vmem),
        compiler_params=limit(8),
        name="rotation",
    )(flag, gram_total)


def vmem():
    return pl.BlockSpec(memory_space=pltpu.VMEM)


def smem():
    return pl.BlockSpec(memory_space=pltpu.SMEM)


def limit(megabytes):
    return pltpu.CompilerParams(vmem_limit_bytes=megabytes * 2**20)


def tile_rows(tile, size):
    return pl.ds(pl.multiple_of(tile * size, size), size)


def gram_kernel(x_ref, out_ref, sent_ref, rest_ref, held, sems, sent_sems):
    size = 2 * TILE
    places, copies, sends = [], [], []
    for tile in range(x_ref.shape[0] // size):
        rows = pl.ds(tile * size, size)
        place = held.at[rows] if tile < RAW_TILES else rest_ref.at[pl.ds((tile - RAW_TILES) * size, size)]
        places.append(place)
        copies.append(pltpu.make_async_copy(x_ref.at[rows], place, sems.at[tile]))
        if tile < RAW_TILES:
            sends.append(pltpu.make_async_copy(place, sent_ref.at[rows], sent_sems.at[tile]))
    for copy in copies:
        copy.start()
    total = jnp.zeros((ORDER, 2 * ORDER), F32)
    for tile, copy in enumerate(copies):
        copy.wait()
        if tile < RAW_TILES:
            sends[tile].start()
        high, low = split_two(places[tile][...])
        total = total + dot_bf16(high, jnp.concatenate([high, low], axis=1), ((0,), (0,)))
    mixed = total[:, ORDER:]
    out_ref[...] = total[:, :ORDER] + (mixed + mixed.T)
    for send in sends:
        send.wait()


def gram_and_rows(columns):
    rows = columns.shape[0]
    tiles = rows // (2 * TILE)
    raw_rows = RAW_TILES * 2 * TILE
    return pl.pallas_call(
        gram_kernel,
        out_shape=(
            jax.ShapeDtypeStruct((ORDER, ORDER), F32),
            jax.ShapeDtypeStruct((raw_rows, ORDER), F32),
            jax.ShapeDtypeStruct((rows - raw_rows, ORDER), F32),
        ),
        in_specs=[pl.BlockSpec(memory_space=pl.ANY)],
        out_specs=(vmem(), pl.BlockSpec(memory_space=pl.ANY), vmem()),
        scratch_shapes=[
            pltpu.VMEM((raw_rows, ORDER), F32),
            pltpu.SemaphoreType.DMA((tiles,)),
            pltpu.SemaphoreType.DMA((RAW_TILES,)),
        ],
        compiler_params=limit(GRAM_LIMIT),
        name="gram",
    )(columns)


def store_weights(weights, high, low):
    high[...], low[...] = split_two(weights)


def dot_three(value, high, low):
    value_high, value_low = split_two(value)
    dims = ((1,), (0,))
    width = high.shape[1]
    if width > ORDER:
        small = dot_bf16(value_high, low[...], dims) + dot_bf16(value_low, high[...], dims)
        return dot_bf16(value_high, high[...], dims) + small
    both = dot_bf16(value_high, jnp.concatenate([high[...], low[...]], axis=1), dims)
    return both[:, :width] + (both[:, width:] + dot_bf16(value_low, high[...], dims))


def packed(ref, tile):
    return jnp.concatenate([ref[tile_rows(2 * tile, TILE)], ref[tile_rows(2 * tile + 1, TILE)]], axis=1)


def turn_kernel(flag_ref, rows_ref, x_ref, early_ref, late_ref, high, low):
    front, back = rows_ref[:HALF], rows_ref[HALF:]
    is_back = flag_ref[0] == 1
    early = jnp.where(is_back, back, front)
    late = jnp.where(is_back, front, back)
    none = jnp.zeros_like(early)
    upper = jnp.concatenate([early, none, late, none], axis=0)
    lower = jnp.concatenate([none, early, none, late], axis=0)
    store_weights(jnp.concatenate([upper, lower], axis=1).T, high, low)

    @pl.loop(0, early_ref.shape[0] // TILE)
    def _(tile):
        out = dot_three(packed(x_ref, tile), high, low)
        early_ref[tile_rows(tile, TILE)] = out[:, :ORDER]
        late_ref[tile_rows(tile, TILE)] = out[:, ORDER:]


def turn(columns, turn_rows, early_is_back):
    half = jax.ShapeDtypeStruct((columns.shape[0] // 2, ORDER), F32)
    return pl.pallas_call(
        turn_kernel,
        out_shape=(half, half),
        in_specs=[smem(), vmem(), vmem()],
        out_specs=(vmem(), vmem()),
        scratch_shapes=[pltpu.VMEM((2 * ORDER, 2 * ORDER), BF16)] * 2,
        compiler_params=limit(16),
        name="turn",
    )(early_is_back, turn_rows, columns)


def turn_raw_kernel(rows_ref, x_ref, out_ref, high, low):
    rows = rows_ref[...]
    none = jnp.zeros_like(rows)
    upper = jnp.concatenate([rows, none], axis=0)
    lower = jnp.concatenate([none, rows], axis=0)
    store_weights(jnp.concatenate([upper, lower], axis=1).T, high, low)

    @pl.loop(0, out_ref.shape[0] // TILE)
    def _(tile):
        out_ref[tile_rows(tile, TILE)] = dot_three(packed(x_ref, tile), high, low)


def turn_raw(columns, half_rows):
    return pl.pallas_call(
        turn_raw_kernel,
        out_shape=jax.ShapeDtypeStruct((columns.shape[0] // 2, ORDER), F32),
        in_specs=[vmem(), vmem()],
        out_specs=vmem(),
        scratch_shapes=[pltpu.VMEM((2 * ORDER, ORDER), BF16)] * 2,
        compiler_params=limit(16),
        name="turn_raw",
    )(half_rows, columns)


def half_roll(value, axis):
    return pltpu.roll(value, HALF, axis)


def low_lanes(shape):
    return lax.broadcasted_iota(jnp.int32, shape, 1) < HALF


def pair_gram_kernel(core_ref, before_ref, own_ref, come_ref, out_ref, total):
    total[...] = jnp.zeros_like(total)

    @pl.loop(0, own_ref.shape[0] // TILE)
    def _(tile):
        rows = tile_rows(tile, TILE)
        high, low = split_two(jnp.concatenate([own_ref[rows], come_ref[rows]], axis=1))
        total[...] += dot_bf16(high, jnp.concatenate([high, low], axis=1), ((0,), (0,)))

    mixed = total[:, 2 * ORDER :]
    whole = total[:, : 2 * ORDER] + (mixed + mixed.T)
    tops = jnp.concatenate([whole[:HALF], whole[ORDER : ORDER + HALF]], axis=0)
    bottoms = jnp.concatenate([whole[HALF:ORDER], whole[ORDER + HALF :]], axis=0)
    first = low_lanes((ORDER, ORDER))
    gram = jnp.where(first, tops[:, :ORDER], half_roll(tops[:, ORDER:], 1)) + jnp.where(
        first, half_roll(bottoms[:, :ORDER], 1), bottoms[:, ORDER:]
    )
    swapped = half_roll(half_roll(gram, 1), 0)
    out_ref[...] = before_ref[...] + jnp.where(core_ref[0] == 1, swapped, gram)


def pair_gram(core, before, own, come):
    return pl.pallas_call(
        pair_gram_kernel,
        out_shape=jax.ShapeDtypeStruct((ORDER, ORDER), F32),
        in_specs=[smem(), vmem(), vmem(), vmem()],
        out_specs=vmem(),
        scratch_shapes=[pltpu.VMEM((2 * ORDER, 4 * ORDER), F32)],
        compiler_params=limit(16),
        name="pair_gram",
    )(core, before, own, come)


def finish_kernel(places, flags_ref, mine_ref, other_ref, *refs):
    parts, (out_ref, early_high, early_low, late_high, late_low, held, sems) = refs[:-7], refs[-7:]
    swap = flags_ref[1] == 1

    def ordered(rows):
        return jnp.where(swap, half_roll(half_roll(rows, 1), 0), rows)

    first = low_lanes((HALF, ORDER))
    late_rows = ordered(mine_ref[...])[:HALF]
    early_rows = ordered(other_ref[...])[HALF:]
    late_own, late_come = jnp.where(first, late_rows, 0.0), jnp.where(first, 0.0, late_rows)
    early_last, early_own = jnp.where(first, early_rows, 0.0), jnp.where(first, 0.0, early_rows)

    def store(upper, lower, lower_first, high, low):
        above = jnp.where(lower_first, lower, upper)
        below = jnp.where(lower_first, upper, lower)
        store_weights(jnp.concatenate([above, below], axis=0).T, high, low)

    is_back = flags_ref[0] == 1
    store(
        jnp.concatenate([half_roll(early_own, 1), early_last], axis=1),
        jnp.concatenate([early_own, half_roll(early_last, 1)], axis=1),
        is_back,
        early_high,
        early_low,
    )
    store(
        jnp.concatenate([late_own, half_roll(late_come, 1)], axis=1),
        jnp.concatenate([half_roll(late_own, 1), late_come], axis=1),
        jnp.logical_not(is_back),
        late_high,
        late_low,
    )
    late_lanes = low_lanes((TILE, ORDER)) == is_back

    def out_copy(tile):
        size = 2 * TILE
        return pltpu.make_async_copy(held.at[tile], out_ref.at[tile_rows(tile, size)], sems.at[tile])

    for index, (place, tiles) in enumerate(places):
        early_ref, late_ref, come_ref, last_ref = parts[4 * index : 4 * index + 4]

        @pl.loop(0, tiles)
        def _(tile):
            rows = tile_rows(tile, TILE)
            early = jnp.concatenate([early_ref[rows], last_ref[rows]], axis=1)
            late = jnp.concatenate([late_ref[rows], come_ref[rows]], axis=1)
            early = dot_three(early, early_high, early_low)
            late = dot_three(late, late_high, late_low)
            held[tile + place, :TILE] = jnp.where(late_lanes, late, early)
            held[tile + place, TILE:] = half_roll(jnp.where(late_lanes, early, late), 1)
            out_copy(tile + place).start()

    for tile in range(held.shape[0]):
        out_copy(tile).wait()


def finish(flags, mine, other, places, parts, rows):
    tiles = rows // (2 * TILE)
    return pl.pallas_call(
        functools.partial(finish_kernel, places),
        out_shape=jax.ShapeDtypeStruct((rows, ORDER), F32),
        in_specs=[smem()] + [vmem()] * (2 + len(parts)),
        out_specs=pl.BlockSpec(memory_space=pl.ANY),
        scratch_shapes=[
            pltpu.VMEM((2 * ORDER, ORDER), BF16),
            pltpu.VMEM((2 * ORDER, ORDER), BF16),
            pltpu.VMEM((2 * ORDER, ORDER), BF16),
            pltpu.VMEM((2 * ORDER, ORDER), BF16),
            pltpu.VMEM((tiles, 2 * TILE, ORDER), F32),
            pltpu.SemaphoreType.DMA((tiles,)),
        ],
        compiler_params=limit(24),
        name="finish",
    )(flags, mine, other, *parts)


def moved(array, target):
    rows, cols = lax.axis_size("row"), lax.axis_size("col")
    pairs = []
    for row in range(rows):
        for col in range(cols):
            to_row, to_col = target(row, col)
            pairs.append((row * cols + col, (to_row % rows) * cols + to_col % cols))
    return lax.ppermute(array, ("row", "col"), pairs)


def outward(row, col):
    return row, col + (1 if row % 2 == 0 else -1)


def inward(row, col):
    return row, col + (-1 if row % 2 == 0 else 1)


def inward_swapped(row, col):
    to_row, to_col = inward(row, col)
    return to_row ^ 1, to_col


def swap_rows(by):
    return lambda row, col: (row ^ by, col)


def summed(gram):
    for by in (2, 4, 8):
        gram = gram + moved(gram, swap_rows(by))
    return gram


def tied(first, *others):
    return lax.optimization_barrier((first, *others))[0]


def local(matrix, plan):
    rows = matrix.shape[0]
    tiles = rows // (2 * TILE)
    core = lax.axis_index("row") % 2
    leaver = plan[lax.axis_index("col")]
    early_is_back = leaver ^ core
    flag, core_flag = early_is_back.reshape(1), core.reshape(1)
    rest_tiles = tiles - RAW_TILES
    places = ((0, RAW_TILES), (RAW_TILES, rest_tiles))

    gram, sent, rest = gram_and_rows(matrix)
    raw_come = moved(sent, outward)
    gram = gram + moved(gram, swap_rows(1))
    first_turn, half_turn = rotation_rows(flag, summed(gram))
    come_turn = moved(half_turn, inward_swapped)

    early_b, late_b = turn(rest, first_turn, flag)
    come_b = moved(early_b, outward)
    early_a, late_a = turn(sent, tied(first_turn, early_b, come_turn), flag)
    come_a = turn_raw(raw_come, come_turn)
    second = pair_gram(core_flag, jnp.zeros_like(gram), late_a, come_a)
    second = pair_gram(core_flag, second, late_b, come_b)
    last_a = moved(tied(late_a, come_b), inward)
    last_b = moved(tied(late_b, come_b, come_turn), inward)
    second = second + moved(moved(second, swap_rows(1)), outward)
    mine, _ = rotation_rows(flag, summed(second))
    other = moved(mine, swap_rows(1))
    flags = jnp.stack([early_is_back, core])
    parts = [early_a, late_a, come_a, last_a, early_b, late_b, come_b, last_b]
    return finish(flags, mine, other, places, parts, rows)


def solution(mesh):
    in_specs = (P("row", "col"), P())
    out_specs = P("row", "col")
    return jax.shard_map(local, mesh=mesh, in_specs=in_specs, out_specs=out_specs, check_vma=False)
```

```python
import functools

import jax
import jax.numpy as jnp
from jax import lax
from jax.experimental import pallas as pl
from jax.experimental.pallas import tpu as pltpu
from jax.sharding import PartitionSpec as P

ITERS = 3
ORDER = 128
HALF = 64
GROUP = 8
TILE = 512
RAW_TILES = 6
GRAM_LIMIT = 48
ROTATION_LIMIT = 16
F32 = jnp.float32
BF16 = jnp.bfloat16


def split_two(value):
    high = value.astype(BF16)
    low = (value - high.astype(F32)).astype(BF16)
    return high, low


def split_three(value):
    high = value.astype(BF16)
    rest = value - high.astype(F32)
    middle = rest.astype(BF16)
    low = (rest - middle.astype(F32)).astype(BF16)
    return high, middle, low


def dot_bf16(left, right, dims):
    return lax.dot_general(left, right, (dims, ((), ())), preferred_element_type=F32)


def dot_six(left, right, transpose_right):
    lh, lm, ll = split_three(left)
    rh, rm, rl = split_three(right)
    axis = 1 if transpose_right else 0
    dims = ((1,), (axis,))
    total = None
    for (la, ra), (lb, rb) in (((lh, rl), (ll, rh)), ((lm, rm), (lm, rh)), ((lh, rm), (lh, rh))):
        term = dot_bf16(
            jnp.concatenate([la, lb], axis=1), jnp.concatenate([ra, rb], axis=axis), dims
        )
        total = term if total is None else total + term
    return total


def across(column, rows):
    return jnp.broadcast_to(column, (rows, ORDER))


def orthonormal_rows(normal, rows_in):
    done = []
    spot = lax.broadcasted_iota(jnp.int32, (GROUP, ORDER), 0)
    head_c = [across(normal[:GROUP, j : j + 1], GROUP) for j in range(GROUP)]
    for start in range(0, ORDER, GROUP):
        tail, after = ORDER - start - GROUP, start + GROUP
        head_n, head_y = normal[:GROUP], rows_in[:GROUP]
        tail_n, tail_y = normal[GROUP:], rows_in[GROUP:]
        tail_c, next_c = [], []
        if tail:
            tail_c = [across(tail_n[:, start + j : start + j + 1], tail) for j in range(GROUP)]
            next_c = [across(tail_n[:GROUP, after + j : after + j + 1], GROUP) for j in range(GROUP)]
        pivots = None
        for k in range(GROUP):
            pivot = across(head_c[k][k : k + 1], GROUP)
            inverse = 1.0 / pivot
            row_n = head_n[k : k + 1]
            row_y = head_y[k : k + 1]
            pivots = jnp.where(spot >= k, pivot, pivots) if k else pivot
            cross = [head_c[j][k : k + 1] for j in range(k + 1, GROUP)]
            if k < GROUP - 1:
                scaled = jnp.where(spot > k, head_c[k] * inverse, 0.0)
                for j in range(k + 1, GROUP):
                    head_c[j] = head_c[j] - scaled * cross[j - k - 1]
                if tail:
                    head_n = head_n - scaled * row_n
                head_y = head_y - scaled * row_y
            if tail:
                column = tail_c[k]
                scaled = column * inverse[:1]
                for j in range(k + 1, GROUP):
                    tail_c[j] = tail_c[j] - scaled * cross[j - k - 1]
                for j in range(GROUP):
                    next_c[j] = next_c[j] - scaled[:GROUP] * column[j : j + 1]
                if tail > GROUP:
                    tail_n = tail_n - scaled * row_n
                tail_y = tail_y - scaled * row_y
        done.append(head_y * lax.rsqrt(pivots))
        normal, rows_in, head_c = tail_n, tail_y, next_c
    return jnp.concatenate(done, axis=0)


def rotation_kernel(flag_ref, gram_ref, *refs):
    out_ref, half_ref = refs[-2:]
    gram = gram_ref[...]
    gram = gram * (1.0 / jnp.max(jnp.abs(gram)))

    def turn(rows):
        out_ref[...] = orthonormal_rows(dot_six(rows, rows, True), rows)

    turn(gram)

    def step(_, carry):
        turn(dot_six(out_ref[...], gram, False))
        return carry

    lax.fori_loop(1, ITERS, step, 0)
    half_ref[...] = jnp.where(flag_ref[0] == 1, out_ref[:HALF], out_ref[HALF:])


def rotation_rows(flag, gram_total, *beside):
    vmem = pl.BlockSpec(memory_space=pltpu.VMEM)
    return pl.pallas_call(
        rotation_kernel,
        out_shape=(
            jax.ShapeDtypeStruct((ORDER, ORDER), F32),
            jax.ShapeDtypeStruct((HALF, ORDER), F32),
        ),
        in_specs=[pl.BlockSpec(memory_space=pltpu.SMEM), vmem] + [vmem] * len(beside),
        out_specs=(vmem, vmem),
        compiler_params=limit(ROTATION_LIMIT),
        name="rotation",
    )(flag, gram_total, *beside)


def vmem():
    return pl.BlockSpec(memory_space=pltpu.VMEM)


def smem():
    return pl.BlockSpec(memory_space=pltpu.SMEM)


def limit(megabytes):
    return pltpu.CompilerParams(vmem_limit_bytes=megabytes * 2**20)


def tile_rows(tile, size):
    return pl.ds(pl.multiple_of(tile * size, size), size)


def cost(flops, moved_bytes):
    return pl.CostEstimate(flops=flops, bytes_accessed=moved_bytes, transcendentals=0)


def gram_kernel(x_ref, out_ref, sent_ref, rest_ref, held, sems, sent_sems):
    size = 2 * TILE
    places, copies, sends = [], [], []
    for tile in range(x_ref.shape[0] // size):
        rows = pl.ds(tile * size, size)
        place = held.at[rows] if tile < RAW_TILES else rest_ref.at[pl.ds((tile - RAW_TILES) * size, size)]
        places.append(place)
        copies.append(pltpu.make_async_copy(x_ref.at[rows], place, sems.at[tile]))
        if tile < RAW_TILES:
            sends.append(pltpu.make_async_copy(place, sent_ref.at[rows], sent_sems.at[tile]))
    for copy in copies:
        copy.start()
    total = jnp.zeros((ORDER, 2 * ORDER), F32)
    for tile, copy in enumerate(copies):
        copy.wait()
        if tile < RAW_TILES:
            sends[tile].start()
        high, low = split_two(places[tile][...])
        total = total + dot_bf16(high, jnp.concatenate([high, low], axis=1), ((0,), (0,)))
    mixed = total[:, ORDER:]
    out_ref[...] = total[:, :ORDER] + (mixed + mixed.T)
    for send in sends:
        send.wait()


def gram_and_rows(columns):
    rows = columns.shape[0]
    tiles = rows // (2 * TILE)
    raw_rows = RAW_TILES * 2 * TILE
    return pl.pallas_call(
        gram_kernel,
        out_shape=(
            jax.ShapeDtypeStruct((ORDER, ORDER), F32),
            jax.ShapeDtypeStruct((raw_rows, ORDER), F32),
            jax.ShapeDtypeStruct((rows - raw_rows, ORDER), F32),
        ),
        in_specs=[pl.BlockSpec(memory_space=pl.ANY)],
        out_specs=(vmem(), pl.BlockSpec(memory_space=pl.ANY), vmem()),
        scratch_shapes=[
            pltpu.VMEM((raw_rows, ORDER), F32),
            pltpu.SemaphoreType.DMA((tiles,)),
            pltpu.SemaphoreType.DMA((RAW_TILES,)),
        ],
        compiler_params=limit(GRAM_LIMIT),
        cost_estimate=cost(4 * rows * ORDER * ORDER, 4 * rows * ORDER),
        name="gram",
    )(columns)


def store_weights(weights, high, low):
    high[...], low[...] = split_two(weights)


def dot_three(value, high, low):
    value_high, value_low = split_two(value)
    dims = ((1,), (0,))
    width = high.shape[1]
    if width > ORDER:
        small = dot_bf16(value_high, low[...], dims) + dot_bf16(value_low, high[...], dims)
        return dot_bf16(value_high, high[...], dims) + small
    both = dot_bf16(value_high, jnp.concatenate([high[...], low[...]], axis=1), dims)
    return both[:, :width] + (both[:, width:] + dot_bf16(value_low, high[...], dims))


def packed(ref, tile):
    return jnp.concatenate([ref[tile_rows(2 * tile, TILE)], ref[tile_rows(2 * tile + 1, TILE)]], axis=1)


def turn_kernel(flag_ref, rows_ref, x_ref, early_ref, late_ref, high, low):
    front, back = rows_ref[:HALF], rows_ref[HALF:]
    is_back = flag_ref[0] == 1
    early = jnp.where(is_back, back, front)
    late = jnp.where(is_back, front, back)
    none = jnp.zeros_like(early)
    upper = jnp.concatenate([early, none, late, none], axis=0)
    lower = jnp.concatenate([none, early, none, late], axis=0)
    store_weights(jnp.concatenate([upper, lower], axis=1).T, high, low)

    @pl.loop(0, early_ref.shape[0] // TILE, unroll=True)
    def _(tile):
        out = dot_three(packed(x_ref, tile), high, low)
        early_ref[tile_rows(tile, TILE)] = out[:, :ORDER]
        late_ref[tile_rows(tile, TILE)] = out[:, ORDER:]


def turn(columns, turn_rows, early_is_back):
    half = jax.ShapeDtypeStruct((columns.shape[0] // 2, ORDER), F32)
    return pl.pallas_call(
        turn_kernel,
        out_shape=(half, half),
        in_specs=[smem(), vmem(), vmem()],
        out_specs=(vmem(), vmem()),
        scratch_shapes=[pltpu.VMEM((2 * ORDER, 2 * ORDER), BF16)] * 2,
        compiler_params=limit(16),
        cost_estimate=cost(12 * columns.shape[0] * ORDER * ORDER, 8 * columns.shape[0] * ORDER),
        name="turn",
    )(early_is_back, turn_rows, columns)


def turn_raw_kernel(rows_ref, x_ref, out_ref, high, low):
    rows = rows_ref[...]
    none = jnp.zeros_like(rows)
    upper = jnp.concatenate([rows, none], axis=0)
    lower = jnp.concatenate([none, rows], axis=0)
    store_weights(jnp.concatenate([upper, lower], axis=1).T, high, low)

    @pl.loop(0, out_ref.shape[0] // TILE, unroll=True)
    def _(tile):
        out_ref[tile_rows(tile, TILE)] = dot_three(packed(x_ref, tile), high, low)


def turn_raw(columns, half_rows):
    return pl.pallas_call(
        turn_raw_kernel,
        out_shape=jax.ShapeDtypeStruct((columns.shape[0] // 2, ORDER), F32),
        in_specs=[vmem(), vmem()],
        out_specs=vmem(),
        scratch_shapes=[pltpu.VMEM((2 * ORDER, ORDER), BF16)] * 2,
        compiler_params=limit(16),
        cost_estimate=cost(8 * columns.shape[0] * ORDER * ORDER, 6 * columns.shape[0] * ORDER),
        name="turn_raw",
    )(half_rows, columns)


def half_roll(value, axis):
    return pltpu.roll(value, HALF, axis)


def low_lanes(shape):
    return lax.broadcasted_iota(jnp.int32, shape, 1) < HALF


def pair_gram_kernel(core_ref, before_ref, own_ref, come_ref, out_ref, total):
    total[...] = jnp.zeros_like(total)

    @pl.loop(0, own_ref.shape[0] // TILE, unroll=True)
    def _(tile):
        rows = tile_rows(tile, TILE)
        high, low = split_two(jnp.concatenate([own_ref[rows], come_ref[rows]], axis=1))
        total[...] += dot_bf16(high, jnp.concatenate([high, low], axis=1), ((0,), (0,)))

    mixed = total[:, 2 * ORDER :]
    whole = total[:, : 2 * ORDER] + (mixed + mixed.T)
    tops = jnp.concatenate([whole[:HALF], whole[ORDER : ORDER + HALF]], axis=0)
    bottoms = jnp.concatenate([whole[HALF:ORDER], whole[ORDER + HALF :]], axis=0)
    first = low_lanes((ORDER, ORDER))
    gram = jnp.where(first, tops[:, :ORDER], half_roll(tops[:, ORDER:], 1)) + jnp.where(
        first, half_roll(bottoms[:, :ORDER], 1), bottoms[:, ORDER:]
    )
    swapped = half_roll(half_roll(gram, 1), 0)
    out_ref[...] = before_ref[...] + jnp.where(core_ref[0] == 1, swapped, gram)


def pair_gram(core, before, own, come):
    return pl.pallas_call(
        pair_gram_kernel,
        out_shape=jax.ShapeDtypeStruct((ORDER, ORDER), F32),
        in_specs=[smem(), vmem(), vmem(), vmem()],
        out_specs=vmem(),
        scratch_shapes=[pltpu.VMEM((2 * ORDER, 4 * ORDER), F32)],
        compiler_params=limit(16),
        cost_estimate=cost(16 * own.shape[0] * ORDER * ORDER, 8 * own.shape[0] * ORDER),
        name="pair_gram",
    )(core, before, own, come)


def finish_kernel(places, flags_ref, mine_ref, other_ref, *refs):
    parts, (out_ref, early_high, early_low, late_high, late_low, held, sems) = refs[:-7], refs[-7:]
    swap = flags_ref[1] == 1

    def ordered(rows):
        return jnp.where(swap, half_roll(half_roll(rows, 1), 0), rows)

    first = low_lanes((HALF, ORDER))
    late_rows = ordered(mine_ref[...])[:HALF]
    early_rows = ordered(other_ref[...])[HALF:]
    late_own, late_come = jnp.where(first, late_rows, 0.0), jnp.where(first, 0.0, late_rows)
    early_last, early_own = jnp.where(first, early_rows, 0.0), jnp.where(first, 0.0, early_rows)

    def store(upper, lower, lower_first, high, low):
        above = jnp.where(lower_first, lower, upper)
        below = jnp.where(lower_first, upper, lower)
        store_weights(jnp.concatenate([above, below], axis=0).T, high, low)

    is_back = flags_ref[0] == 1
    store(
        jnp.concatenate([half_roll(early_own, 1), early_last], axis=1),
        jnp.concatenate([early_own, half_roll(early_last, 1)], axis=1),
        is_back,
        early_high,
        early_low,
    )
    store(
        jnp.concatenate([late_own, half_roll(late_come, 1)], axis=1),
        jnp.concatenate([half_roll(late_own, 1), late_come], axis=1),
        jnp.logical_not(is_back),
        late_high,
        late_low,
    )
    late_lanes = low_lanes((TILE, ORDER)) == is_back

    def out_copy(tile):
        size = 2 * TILE
        return pltpu.make_async_copy(held.at[tile], out_ref.at[tile_rows(tile, size)], sems.at[tile])

    for index, (place, tiles) in enumerate(places):
        early_ref, late_ref, come_ref, last_ref = parts[4 * index : 4 * index + 4]

        @pl.loop(0, tiles, unroll=True)
        def _(tile):
            rows = tile_rows(tile, TILE)
            early = jnp.concatenate([early_ref[rows], last_ref[rows]], axis=1)
            late = jnp.concatenate([late_ref[rows], come_ref[rows]], axis=1)
            early = dot_three(early, early_high, early_low)
            late = dot_three(late, late_high, late_low)
            held[tile + place, :TILE] = jnp.where(late_lanes, late, early)
            held[tile + place, TILE:] = half_roll(jnp.where(late_lanes, early, late), 1)
            out_copy(tile + place).start()

    for tile in range(held.shape[0]):
        out_copy(tile).wait()


def finish(flags, mine, other, places, parts, rows):
    tiles = rows // (2 * TILE)
    return pl.pallas_call(
        functools.partial(finish_kernel, places),
        out_shape=jax.ShapeDtypeStruct((rows, ORDER), F32),
        in_specs=[smem()] + [vmem()] * (2 + len(parts)),
        out_specs=pl.BlockSpec(memory_space=pl.ANY),
        scratch_shapes=[
            pltpu.VMEM((2 * ORDER, ORDER), BF16),
            pltpu.VMEM((2 * ORDER, ORDER), BF16),
            pltpu.VMEM((2 * ORDER, ORDER), BF16),
            pltpu.VMEM((2 * ORDER, ORDER), BF16),
            pltpu.VMEM((tiles, 2 * TILE, ORDER), F32),
            pltpu.SemaphoreType.DMA((tiles,)),
        ],
        compiler_params=limit(24),
        name="finish",
    )(flags, mine, other, *parts)


def moved(array, target):
    rows, cols = lax.axis_size("row"), lax.axis_size("col")
    pairs = []
    for row in range(rows):
        for col in range(cols):
            to_row, to_col = target(row, col)
            pairs.append((row * cols + col, (to_row % rows) * cols + to_col % cols))
    return lax.ppermute(array, ("row", "col"), pairs)


def outward(row, col):
    return row, col + (1 if row % 2 == 0 else -1)


def inward(row, col):
    return row, col + (-1 if row % 2 == 0 else 1)


def inward_swapped(row, col):
    to_row, to_col = inward(row, col)
    return to_row ^ 1, to_col


def swap_rows(by):
    return lambda row, col: (row ^ by, col)


def summed(gram):
    for by in (2, 4, 8):
        gram = gram + moved(gram, swap_rows(by))
    return gram


def tied(first, *others):
    return lax.optimization_barrier((first, *others))[0]


def local(matrix, plan):
    rows = matrix.shape[0]
    tiles = rows // (2 * TILE)
    core = lax.axis_index("row") % 2
    leaver = plan[lax.axis_index("col")]
    early_is_back = leaver ^ core
    flag, core_flag = early_is_back.reshape(1), core.reshape(1)
    rest_tiles = tiles - RAW_TILES
    places = ((0, RAW_TILES), (RAW_TILES, rest_tiles))

    gram, sent, rest = gram_and_rows(matrix)
    raw_come = moved(sent, outward)
    gram = gram + moved(gram, swap_rows(1))
    first_turn, half_turn = rotation_rows(flag, summed(gram), rest)
    come_turn = moved(half_turn, inward_swapped)

    early_b, late_b = turn(rest, first_turn, flag)
    come_b = moved(early_b, outward)
    early_a, late_a = turn(sent, tied(first_turn, early_b, come_turn), flag)
    come_a = turn_raw(raw_come, come_turn)
    second = pair_gram(core_flag, jnp.zeros_like(gram), late_a, come_a)
    second = pair_gram(core_flag, second, late_b, come_b)
    last_a = moved(tied(late_a, second), inward)
    last_b = moved(tied(late_b, second), inward)
    second = second + moved(moved(second, swap_rows(1)), outward)
    mine, _ = rotation_rows(flag, summed(second))
    other = moved(mine, swap_rows(1))
    flags = jnp.stack([early_is_back, core])
    parts = [early_a, late_a, come_a, last_a, early_b, late_b, come_b, last_b]
    return finish(flags, mine, other, places, parts, rows)


def solution(mesh):
    in_specs = (P("row", "col"), P())
    out_specs = P("row", "col")
    return jax.shard_map(local, mesh=mesh, in_specs=in_specs, out_specs=out_specs, check_vma=False)
```

```python
import functools

import jax
import jax.numpy as jnp
from jax import lax
from jax.experimental import pallas as pl
from jax.experimental.pallas import tpu as pltpu
from jax.sharding import PartitionSpec as P

ITERS = 3
ORDER = 128
HALF = 64
GROUP = 8
TILE = 512
RAW_TILES = 6
GRAM_LIMIT = 48
ROTATION_LIMIT = 48
F32 = jnp.float32
BF16 = jnp.bfloat16


def split_two(value):
    high = value.astype(BF16)
    low = (value - high.astype(F32)).astype(BF16)
    return high, low


def split_three(value):
    high = value.astype(BF16)
    rest = value - high.astype(F32)
    middle = rest.astype(BF16)
    low = (rest - middle.astype(F32)).astype(BF16)
    return high, middle, low


def dot_bf16(left, right, dims):
    return lax.dot_general(left, right, (dims, ((), ())), preferred_element_type=F32)


def dot_six(left, right, transpose_right):
    lh, lm, ll = split_three(left)
    rh, rm, rl = split_three(right)
    axis = 1 if transpose_right else 0
    dims = ((1,), (axis,))
    total = None
    for (la, ra), (lb, rb) in (((lh, rl), (ll, rh)), ((lm, rm), (lm, rh)), ((lh, rm), (lh, rh))):
        term = dot_bf16(
            jnp.concatenate([la, lb], axis=1), jnp.concatenate([ra, rb], axis=axis), dims
        )
        total = term if total is None else total + term
    return total


def across(column, rows):
    return jnp.broadcast_to(column, (rows, ORDER))


def orthonormal_rows(normal, rows_in):
    done = []
    spot = lax.broadcasted_iota(jnp.int32, (GROUP, ORDER), 0)
    head_c = [across(normal[:GROUP, j : j + 1], GROUP) for j in range(GROUP)]
    for start in range(0, ORDER, GROUP):
        tail, after = ORDER - start - GROUP, start + GROUP
        head_n, head_y = normal[:GROUP], rows_in[:GROUP]
        tail_n, tail_y = normal[GROUP:], rows_in[GROUP:]
        tail_c, next_c = [], []
        if tail:
            tail_c = [across(tail_n[:, start + j : start + j + 1], tail) for j in range(GROUP)]
            next_c = [across(tail_n[:GROUP, after + j : after + j + 1], GROUP) for j in range(GROUP)]
        pivots = None
        for k in range(GROUP):
            pivot = across(head_c[k][k : k + 1], GROUP)
            inverse = 1.0 / pivot
            row_n = head_n[k : k + 1]
            row_y = head_y[k : k + 1]
            pivots = jnp.where(spot >= k, pivot, pivots) if k else pivot
            cross = [head_c[j][k : k + 1] for j in range(k + 1, GROUP)]
            if k < GROUP - 1:
                scaled = jnp.where(spot > k, head_c[k] * inverse, 0.0)
                for j in range(k + 1, GROUP):
                    head_c[j] = head_c[j] - scaled * cross[j - k - 1]
                if tail:
                    head_n = head_n - scaled * row_n
                head_y = head_y - scaled * row_y
            if tail:
                column = tail_c[k]
                scaled = column * inverse[:1]
                for j in range(k + 1, GROUP):
                    tail_c[j] = tail_c[j] - scaled * cross[j - k - 1]
                for j in range(GROUP):
                    next_c[j] = next_c[j] - scaled[:GROUP] * column[j : j + 1]
                if tail > GROUP:
                    tail_n = tail_n - scaled * row_n
                tail_y = tail_y - scaled * row_y
        done.append(head_y * lax.rsqrt(pivots))
        normal, rows_in, head_c = tail_n, tail_y, next_c
    return jnp.concatenate(done, axis=0)


def rotate(gram, out_ref):
    gram = gram * (1.0 / jnp.max(jnp.abs(gram)))

    def turn_rows(rows):
        out_ref[...] = orthonormal_rows(dot_six(rows, rows, True), rows)

    turn_rows(gram)

    def step(_, carry):
        turn_rows(dot_six(out_ref[...], gram, False))
        return carry

    lax.fori_loop(1, ITERS, step, 0)


def rotation_kernel(gram_ref, out_ref):
    rotate(gram_ref[...], out_ref)


def rotation_rows(gram_total):
    return pl.pallas_call(
        rotation_kernel,
        out_shape=jax.ShapeDtypeStruct((ORDER, ORDER), F32),
        in_specs=[vmem()],
        out_specs=vmem(),
        compiler_params=limit(16),
        name="rotation",
    )(gram_total)


def vmem():
    return pl.BlockSpec(memory_space=pltpu.VMEM)


def smem():
    return pl.BlockSpec(memory_space=pltpu.SMEM)


def limit(megabytes):
    return pltpu.CompilerParams(vmem_limit_bytes=megabytes * 2**20)


def tile_rows(tile, size):
    return pl.ds(pl.multiple_of(tile * size, size), size)


def cost(flops, moved_bytes):
    return pl.CostEstimate(flops=flops, bytes_accessed=moved_bytes, transcendentals=0)


def gram_kernel(x_ref, out_ref, sent_ref, held, sems, sent_sems):
    size = 2 * TILE
    copies, sends = [], []
    for tile in range(held.shape[0]):
        rows = pl.ds(tile * size, size)
        copies.append(pltpu.make_async_copy(x_ref.at[rows], held.at[tile], sems.at[tile]))
        if tile < RAW_TILES:
            sends.append(pltpu.make_async_copy(held.at[tile], sent_ref.at[rows], sent_sems.at[tile]))
    for copy in copies:
        copy.start()
    total = jnp.zeros((ORDER, 2 * ORDER), F32)
    for tile, copy in enumerate(copies):
        copy.wait()
        if tile < RAW_TILES:
            sends[tile].start()
        high, low = split_two(held[tile])
        total = total + dot_bf16(high, jnp.concatenate([high, low], axis=1), ((0,), (0,)))
    mixed = total[:, ORDER:]
    out_ref[...] = total[:, :ORDER] + (mixed + mixed.T)
    for send in sends:
        send.wait()


def gram_and_raw(columns):
    rows = columns.shape[0]
    tiles = rows // (2 * TILE)
    return pl.pallas_call(
        gram_kernel,
        out_shape=(
            jax.ShapeDtypeStruct((ORDER, ORDER), F32),
            jax.ShapeDtypeStruct((RAW_TILES * 2 * TILE, ORDER), F32),
        ),
        in_specs=[pl.BlockSpec(memory_space=pl.ANY)],
        out_specs=(vmem(), pl.BlockSpec(memory_space=pl.ANY)),
        scratch_shapes=[
            pltpu.VMEM((tiles, 2 * TILE, ORDER), F32),
            pltpu.SemaphoreType.DMA((tiles,)),
            pltpu.SemaphoreType.DMA((RAW_TILES,)),
        ],
        compiler_params=limit(GRAM_LIMIT),
        cost_estimate=cost(4 * rows * ORDER * ORDER, 4 * rows * ORDER),
        name="gram",
    )(columns)


def store_weights(weights, high, low):
    high[...], low[...] = split_two(weights)


def dot_three(value, high, low):
    value_high, value_low = split_two(value)
    dims = ((1,), (0,))
    width = high.shape[1]
    if width > ORDER:
        small = dot_bf16(value_high, low[...], dims) + dot_bf16(value_low, high[...], dims)
        return dot_bf16(value_high, high[...], dims) + small
    both = dot_bf16(value_high, jnp.concatenate([high[...], low[...]], axis=1), dims)
    return both[:, :width] + (both[:, width:] + dot_bf16(value_low, high[...], dims))


def packed(ref, tile):
    return jnp.concatenate([ref[tile_rows(2 * tile, TILE)], ref[tile_rows(2 * tile + 1, TILE)]], axis=1)


def turn_weights(rows_ref, is_back, high, low):
    front, back = rows_ref[:HALF], rows_ref[HALF:]
    early = jnp.where(is_back, back, front)
    late = jnp.where(is_back, front, back)
    none = jnp.zeros_like(early)
    upper = jnp.concatenate([early, none, late, none], axis=0)
    lower = jnp.concatenate([none, early, none, late], axis=0)
    store_weights(jnp.concatenate([upper, lower], axis=1).T, high, low)


def turn_tiles(x_ref, early_ref, late_ref, high, low):
    @pl.loop(0, early_ref.shape[0] // TILE, unroll=True)
    def _(tile):
        out = dot_three(packed(x_ref, tile), high, low)
        early_ref[tile_rows(tile, TILE)] = out[:, :ORDER]
        late_ref[tile_rows(tile, TILE)] = out[:, ORDER:]


def turn_kernel(flag_ref, rows_ref, x_ref, early_ref, late_ref, high, low):
    turn_weights(rows_ref, flag_ref[0] == 1, high, low)
    turn_tiles(x_ref, early_ref, late_ref, high, low)


def rotation_turn_kernel(flag_ref, gram_ref, x_ref, rows_ref, half_ref, early_ref, late_ref, high, low, held, sem):
    first = x_ref.shape[0] - held.shape[0]
    copy = pltpu.make_async_copy(x_ref.at[pl.ds(first, held.shape[0])], held, sem)
    copy.start()
    rotate(gram_ref[...], rows_ref)
    is_back = flag_ref[0] == 1
    half_ref[...] = jnp.where(is_back, rows_ref[:HALF], rows_ref[HALF:])
    turn_weights(rows_ref, is_back, high, low)
    copy.wait()
    turn_tiles(held, early_ref, late_ref, high, low)


def rotation_turn(flag, gram_total, columns):
    rows = columns.shape[0] - RAW_TILES * 2 * TILE
    half = jax.ShapeDtypeStruct((rows // 2, ORDER), F32)
    return pl.pallas_call(
        rotation_turn_kernel,
        out_shape=(
            jax.ShapeDtypeStruct((ORDER, ORDER), F32),
            jax.ShapeDtypeStruct((HALF, ORDER), F32),
            half,
            half,
        ),
        in_specs=[smem(), vmem(), pl.BlockSpec(memory_space=pl.ANY)],
        out_specs=(vmem(), vmem(), vmem(), vmem()),
        scratch_shapes=[
            pltpu.VMEM((2 * ORDER, 2 * ORDER), BF16),
            pltpu.VMEM((2 * ORDER, 2 * ORDER), BF16),
            pltpu.VMEM((rows, ORDER), F32),
            pltpu.SemaphoreType.DMA,
        ],
        compiler_params=limit(ROTATION_LIMIT),
        name="rotation_turn",
    )(flag, gram_total, columns)


def turn(columns, turn_rows, early_is_back):
    half = jax.ShapeDtypeStruct((columns.shape[0] // 2, ORDER), F32)
    return pl.pallas_call(
        turn_kernel,
        out_shape=(half, half),
        in_specs=[smem(), vmem(), vmem()],
        out_specs=(vmem(), vmem()),
        scratch_shapes=[pltpu.VMEM((2 * ORDER, 2 * ORDER), BF16)] * 2,
        compiler_params=limit(16),
        cost_estimate=cost(12 * columns.shape[0] * ORDER * ORDER, 8 * columns.shape[0] * ORDER),
        name="turn",
    )(early_is_back, turn_rows, columns)


def turn_raw_kernel(rows_ref, x_ref, out_ref, high, low):
    rows = rows_ref[...]
    none = jnp.zeros_like(rows)
    upper = jnp.concatenate([rows, none], axis=0)
    lower = jnp.concatenate([none, rows], axis=0)
    store_weights(jnp.concatenate([upper, lower], axis=1).T, high, low)

    @pl.loop(0, out_ref.shape[0] // TILE, unroll=True)
    def _(tile):
        out_ref[tile_rows(tile, TILE)] = dot_three(packed(x_ref, tile), high, low)


def turn_raw(columns, half_rows):
    return pl.pallas_call(
        turn_raw_kernel,
        out_shape=jax.ShapeDtypeStruct((columns.shape[0] // 2, ORDER), F32),
        in_specs=[vmem(), vmem()],
        out_specs=vmem(),
        scratch_shapes=[pltpu.VMEM((2 * ORDER, ORDER), BF16)] * 2,
        compiler_params=limit(16),
        cost_estimate=cost(8 * columns.shape[0] * ORDER * ORDER, 6 * columns.shape[0] * ORDER),
        name="turn_raw",
    )(half_rows, columns)


def half_roll(value, axis):
    return pltpu.roll(value, HALF, axis)


def low_lanes(shape):
    return lax.broadcasted_iota(jnp.int32, shape, 1) < HALF


def pair_gram_kernel(core_ref, before_ref, own_ref, come_ref, out_ref, total):
    total[...] = jnp.zeros_like(total)

    @pl.loop(0, own_ref.shape[0] // TILE, unroll=True)
    def _(tile):
        rows = tile_rows(tile, TILE)
        high, low = split_two(jnp.concatenate([own_ref[rows], come_ref[rows]], axis=1))
        total[...] += dot_bf16(high, jnp.concatenate([high, low], axis=1), ((0,), (0,)))

    mixed = total[:, 2 * ORDER :]
    whole = total[:, : 2 * ORDER] + (mixed + mixed.T)
    tops = jnp.concatenate([whole[:HALF], whole[ORDER : ORDER + HALF]], axis=0)
    bottoms = jnp.concatenate([whole[HALF:ORDER], whole[ORDER + HALF :]], axis=0)
    first = low_lanes((ORDER, ORDER))
    gram = jnp.where(first, tops[:, :ORDER], half_roll(tops[:, ORDER:], 1)) + jnp.where(
        first, half_roll(bottoms[:, :ORDER], 1), bottoms[:, ORDER:]
    )
    swapped = half_roll(half_roll(gram, 1), 0)
    out_ref[...] = before_ref[...] + jnp.where(core_ref[0] == 1, swapped, gram)


def pair_gram(core, before, own, come):
    return pl.pallas_call(
        pair_gram_kernel,
        out_shape=jax.ShapeDtypeStruct((ORDER, ORDER), F32),
        in_specs=[smem(), vmem(), vmem(), vmem()],
        out_specs=vmem(),
        scratch_shapes=[pltpu.VMEM((2 * ORDER, 4 * ORDER), F32)],
        compiler_params=limit(16),
        cost_estimate=cost(16 * own.shape[0] * ORDER * ORDER, 8 * own.shape[0] * ORDER),
        name="pair_gram",
    )(core, before, own, come)


def finish_kernel(places, flags_ref, mine_ref, other_ref, *refs):
    parts, (out_ref, early_high, early_low, late_high, late_low, held, sems) = refs[:-7], refs[-7:]
    swap = flags_ref[1] == 1

    def ordered(rows):
        return jnp.where(swap, half_roll(half_roll(rows, 1), 0), rows)

    first = low_lanes((HALF, ORDER))
    late_rows = ordered(mine_ref[...])[:HALF]
    early_rows = ordered(other_ref[...])[HALF:]
    late_own, late_come = jnp.where(first, late_rows, 0.0), jnp.where(first, 0.0, late_rows)
    early_last, early_own = jnp.where(first, early_rows, 0.0), jnp.where(first, 0.0, early_rows)

    def store(upper, lower, lower_first, high, low):
        above = jnp.where(lower_first, lower, upper)
        below = jnp.where(lower_first, upper, lower)
        store_weights(jnp.concatenate([above, below], axis=0).T, high, low)

    is_back = flags_ref[0] == 1
    store(
        jnp.concatenate([half_roll(early_own, 1), early_last], axis=1),
        jnp.concatenate([early_own, half_roll(early_last, 1)], axis=1),
        is_back,
        early_high,
        early_low,
    )
    store(
        jnp.concatenate([late_own, half_roll(late_come, 1)], axis=1),
        jnp.concatenate([half_roll(late_own, 1), late_come], axis=1),
        jnp.logical_not(is_back),
        late_high,
        late_low,
    )
    late_lanes = low_lanes((TILE, ORDER)) == is_back

    def out_copy(tile):
        size = 2 * TILE
        return pltpu.make_async_copy(held.at[tile], out_ref.at[tile_rows(tile, size)], sems.at[tile])

    for index, (place, tiles) in enumerate(places):
        early_ref, late_ref, come_ref, last_ref = parts[4 * index : 4 * index + 4]

        @pl.loop(0, tiles, unroll=True)
        def _(tile):
            rows = tile_rows(tile, TILE)
            early = jnp.concatenate([early_ref[rows], last_ref[rows]], axis=1)
            late = jnp.concatenate([late_ref[rows], come_ref[rows]], axis=1)
            early = dot_three(early, early_high, early_low)
            late = dot_three(late, late_high, late_low)
            held[tile + place, :TILE] = jnp.where(late_lanes, late, early)
            held[tile + place, TILE:] = half_roll(jnp.where(late_lanes, early, late), 1)
            out_copy(tile + place).start()

    for tile in range(held.shape[0]):
        out_copy(tile).wait()


def finish(flags, mine, other, places, parts, rows):
    tiles = rows // (2 * TILE)
    return pl.pallas_call(
        functools.partial(finish_kernel, places),
        out_shape=jax.ShapeDtypeStruct((rows, ORDER), F32),
        in_specs=[smem()] + [vmem()] * (2 + len(parts)),
        out_specs=pl.BlockSpec(memory_space=pl.ANY),
        scratch_shapes=[
            pltpu.VMEM((2 * ORDER, ORDER), BF16),
            pltpu.VMEM((2 * ORDER, ORDER), BF16),
            pltpu.VMEM((2 * ORDER, ORDER), BF16),
            pltpu.VMEM((2 * ORDER, ORDER), BF16),
            pltpu.VMEM((tiles, 2 * TILE, ORDER), F32),
            pltpu.SemaphoreType.DMA((tiles,)),
        ],
        compiler_params=limit(24),
        name="finish",
    )(flags, mine, other, *parts)


def moved(array, target):
    rows, cols = lax.axis_size("row"), lax.axis_size("col")
    pairs = []
    for row in range(rows):
        for col in range(cols):
            to_row, to_col = target(row, col)
            pairs.append((row * cols + col, (to_row % rows) * cols + to_col % cols))
    return lax.ppermute(array, ("row", "col"), pairs)


def outward(row, col):
    return row, col + (1 if row % 2 == 0 else -1)


def inward(row, col):
    return row, col + (-1 if row % 2 == 0 else 1)


def inward_swapped(row, col):
    to_row, to_col = inward(row, col)
    return to_row ^ 1, to_col


def swap_rows(by):
    return lambda row, col: (row ^ by, col)


def summed(gram):
    for by in (2, 4, 14):
        gram = gram + moved(gram, swap_rows(by))
    return gram


def tied(first, *others):
    return lax.optimization_barrier((first, *others))[0]


def local(matrix, plan):
    rows = matrix.shape[0]
    tiles = rows // (2 * TILE)
    core = lax.axis_index("row") % 2
    leaver = plan[lax.axis_index("col")]
    early_is_back = leaver ^ core
    flag, core_flag = early_is_back.reshape(1), core.reshape(1)
    rest_tiles = tiles - RAW_TILES
    places = ((0, RAW_TILES), (RAW_TILES, rest_tiles))

    gram, sent = gram_and_raw(matrix)
    raw_come = moved(sent, outward)
    gram = gram + moved(gram, swap_rows(1))
    first_turn, half_turn, early_b, late_b = rotation_turn(flag, summed(gram), matrix)
    come_turn = moved(half_turn, inward_swapped)

    come_b = moved(early_b, outward)
    early_a, late_a = turn(sent, tied(first_turn, early_b, come_turn), flag)
    come_a = turn_raw(raw_come, come_turn)
    second = pair_gram(core_flag, jnp.zeros_like(gram), late_a, come_a)
    second = pair_gram(core_flag, second, late_b, come_b)
    last_a = moved(tied(late_a, second), inward)
    last_b = moved(tied(late_b, second), inward)
    second = second + moved(moved(second, swap_rows(1)), outward)
    mine = rotation_rows(summed(second))
    other = moved(mine, swap_rows(1))
    flags = jnp.stack([early_is_back, core])
    parts = [early_a, late_a, come_a, last_a, early_b, late_b, come_b, last_b]
    return finish(flags, mine, other, places, parts, rows)


def solution(mesh):
    in_specs = (P("row", "col"), P())
    out_specs = P("row", "col")
    return jax.shard_map(local, mesh=mesh, in_specs=in_specs, out_specs=out_specs, check_vma=False)
```

```python
import functools

import jax
import jax.numpy as jnp
from jax import lax
from jax.experimental import pallas as pl
from jax.experimental.pallas import tpu as pltpu
from jax.sharding import PartitionSpec as P

ITERS = 3
ORDER = 128
HALF = 64
GROUP = 8
TILE = 256
RAW_TILES = 11
GRAM_LIMIT = 48
ROTATION_LIMIT = 48
F32 = jnp.float32
BF16 = jnp.bfloat16


def split_two(value):
    high = value.astype(BF16)
    low = (value - high.astype(F32)).astype(BF16)
    return high, low


def split_three(value):
    high = value.astype(BF16)
    rest = value - high.astype(F32)
    middle = rest.astype(BF16)
    low = (rest - middle.astype(F32)).astype(BF16)
    return high, middle, low


def dot_bf16(left, right, dims):
    return lax.dot_general(left, right, (dims, ((), ())), preferred_element_type=F32)


def dot_six(left, right, transpose_right):
    lh, lm, ll = split_three(left)
    rh, rm, rl = split_three(right)
    axis = 1 if transpose_right else 0
    dims = ((1,), (axis,))
    total = None
    for (la, ra), (lb, rb) in (((lh, rl), (ll, rh)), ((lm, rm), (lm, rh)), ((lh, rm), (lh, rh))):
        term = dot_bf16(
            jnp.concatenate([la, lb], axis=1), jnp.concatenate([ra, rb], axis=axis), dims
        )
        total = term if total is None else total + term
    return total


def across(column, rows):
    return jnp.broadcast_to(column, (rows, ORDER))


def orthonormal_rows(normal, rows_in):
    done = []
    spot = lax.broadcasted_iota(jnp.int32, (GROUP, ORDER), 0)
    head_c = [across(normal[:GROUP, j : j + 1], GROUP) for j in range(GROUP)]
    for start in range(0, ORDER, GROUP):
        tail, after = ORDER - start - GROUP, start + GROUP
        head_n, head_y = normal[:GROUP], rows_in[:GROUP]
        tail_n, tail_y = normal[GROUP:], rows_in[GROUP:]
        tail_c, next_c = [], []
        if tail:
            tail_c = [across(tail_n[:, start + j : start + j + 1], tail) for j in range(GROUP)]
            next_c = [across(tail_n[:GROUP, after + j : after + j + 1], GROUP) for j in range(GROUP)]
        pivots = None
        for k in range(GROUP):
            pivot = across(head_c[k][k : k + 1], GROUP)
            inverse = 1.0 / pivot
            row_n = head_n[k : k + 1]
            row_y = head_y[k : k + 1]
            pivots = jnp.where(spot >= k, pivot, pivots) if k else pivot
            cross = [head_c[j][k : k + 1] for j in range(k + 1, GROUP)]
            if k < GROUP - 1:
                scaled = jnp.where(spot > k, head_c[k] * inverse, 0.0)
                for j in range(k + 1, GROUP):
                    head_c[j] = head_c[j] - scaled * cross[j - k - 1]
                if tail:
                    head_n = head_n - scaled * row_n
                head_y = head_y - scaled * row_y
            if tail:
                column = tail_c[k]
                scaled = column * inverse[:1]
                for j in range(k + 1, GROUP):
                    tail_c[j] = tail_c[j] - scaled * cross[j - k - 1]
                for j in range(GROUP):
                    next_c[j] = next_c[j] - scaled[:GROUP] * column[j : j + 1]
                if tail > GROUP:
                    tail_n = tail_n - scaled * row_n
                tail_y = tail_y - scaled * row_y
        done.append(head_y * lax.rsqrt(pivots))
        normal, rows_in, head_c = tail_n, tail_y, next_c
    return jnp.concatenate(done, axis=0)


def rotate(gram, out_ref):
    gram = gram * (1.0 / jnp.max(jnp.abs(gram)))

    def turn_rows(rows):
        out_ref[...] = orthonormal_rows(dot_six(rows, rows, True), rows)

    turn_rows(gram)

    def step(_, carry):
        turn_rows(dot_six(out_ref[...], gram, False))
        return carry

    lax.fori_loop(1, ITERS, step, 0)


def rotation_kernel(gram_ref, out_ref):
    rotate(gram_ref[...], out_ref)


def rotation_rows(gram_total):
    return pl.pallas_call(
        rotation_kernel,
        out_shape=jax.ShapeDtypeStruct((ORDER, ORDER), F32),
        in_specs=[vmem()],
        out_specs=vmem(),
        compiler_params=limit(16),
        name="rotation",
    )(gram_total)


def vmem():
    return pl.BlockSpec(memory_space=pltpu.VMEM)


def smem():
    return pl.BlockSpec(memory_space=pltpu.SMEM)


def limit(megabytes):
    return pltpu.CompilerParams(vmem_limit_bytes=megabytes * 2**20)


def tile_rows(tile, size):
    return pl.ds(pl.multiple_of(tile * size, size), size)


def cost(flops, moved_bytes):
    return pl.CostEstimate(flops=flops, bytes_accessed=moved_bytes, transcendentals=0)


def gram_kernel(x_ref, out_ref, sent_ref, held, sems, sent_sems):
    size = 2 * TILE
    copies, sends = [], []
    for tile in range(held.shape[0]):
        rows = pl.ds(tile * size, size)
        copies.append(pltpu.make_async_copy(x_ref.at[rows], held.at[tile], sems.at[tile]))
        if tile < RAW_TILES:
            sends.append(pltpu.make_async_copy(held.at[tile], sent_ref.at[rows], sent_sems.at[tile]))
    for copy in copies:
        copy.start()
    total = jnp.zeros((ORDER, 2 * ORDER), F32)
    for tile, copy in enumerate(copies):
        copy.wait()
        if tile < RAW_TILES:
            sends[tile].start()
        high, low = split_two(held[tile])
        total = total + dot_bf16(high, jnp.concatenate([high, low], axis=1), ((0,), (0,)))
    mixed = total[:, ORDER:]
    out_ref[...] = total[:, :ORDER] + (mixed + mixed.T)
    for send in sends:
        send.wait()


def gram_and_raw(columns):
    rows = columns.shape[0]
    tiles = rows // (2 * TILE)
    return pl.pallas_call(
        gram_kernel,
        out_shape=(
            jax.ShapeDtypeStruct((ORDER, ORDER), F32),
            jax.ShapeDtypeStruct((RAW_TILES * 2 * TILE, ORDER), F32),
        ),
        in_specs=[pl.BlockSpec(memory_space=pl.ANY)],
        out_specs=(vmem(), pl.BlockSpec(memory_space=pl.ANY)),
        scratch_shapes=[
            pltpu.VMEM((tiles, 2 * TILE, ORDER), F32),
            pltpu.SemaphoreType.DMA((tiles,)),
            pltpu.SemaphoreType.DMA((RAW_TILES,)),
        ],
        compiler_params=limit(GRAM_LIMIT),
        cost_estimate=cost(4 * rows * ORDER * ORDER, 4 * rows * ORDER),
        name="gram",
    )(columns)


def store_weights(weights, high, low):
    high[...], low[...] = split_two(weights)


def dot_three(value, high, low):
    value_high, value_low = split_two(value)
    dims = ((1,), (0,))
    width = high.shape[1]
    if width > ORDER:
        small = dot_bf16(value_high, low[...], dims) + dot_bf16(value_low, high[...], dims)
        return dot_bf16(value_high, high[...], dims) + small
    both = dot_bf16(value_high, jnp.concatenate([high[...], low[...]], axis=1), dims)
    return both[:, :width] + (both[:, width:] + dot_bf16(value_low, high[...], dims))


def packed(ref, tile):
    return jnp.concatenate([ref[tile_rows(2 * tile, TILE)], ref[tile_rows(2 * tile + 1, TILE)]], axis=1)


def turn_weights(rows_ref, is_back, high, low):
    front, back = rows_ref[:HALF], rows_ref[HALF:]
    early = jnp.where(is_back, back, front)
    late = jnp.where(is_back, front, back)
    none = jnp.zeros_like(early)
    upper = jnp.concatenate([early, none, late, none], axis=0)
    lower = jnp.concatenate([none, early, none, late], axis=0)
    store_weights(jnp.concatenate([upper, lower], axis=1).T, high, low)


def turn_tiles(x_ref, early_ref, late_ref, high, low):
    @pl.loop(0, early_ref.shape[0] // TILE, unroll=True)
    def _(tile):
        out = dot_three(packed(x_ref, tile), high, low)
        early_ref[tile_rows(tile, TILE)] = out[:, :ORDER]
        late_ref[tile_rows(tile, TILE)] = out[:, ORDER:]


def turn_kernel(flag_ref, rows_ref, x_ref, early_ref, late_ref, high, low):
    turn_weights(rows_ref, flag_ref[0] == 1, high, low)
    turn_tiles(x_ref, early_ref, late_ref, high, low)


def rotation_turn_kernel(flag_ref, gram_ref, x_ref, rows_ref, half_ref, early_ref, late_ref, high, low, held, sem):
    first = x_ref.shape[0] - held.shape[0]
    copy = pltpu.make_async_copy(x_ref.at[pl.ds(first, held.shape[0])], held, sem)
    copy.start()
    rotate(gram_ref[...], rows_ref)
    is_back = flag_ref[0] == 1
    half_ref[...] = jnp.where(is_back, rows_ref[:HALF], rows_ref[HALF:])
    turn_weights(rows_ref, is_back, high, low)
    copy.wait()
    turn_tiles(held, early_ref, late_ref, high, low)


def rotation_turn(flag, gram_total, columns):
    rows = columns.shape[0] - RAW_TILES * 2 * TILE
    half = jax.ShapeDtypeStruct((rows // 2, ORDER), F32)
    return pl.pallas_call(
        rotation_turn_kernel,
        out_shape=(
            jax.ShapeDtypeStruct((ORDER, ORDER), F32),
            jax.ShapeDtypeStruct((HALF, ORDER), F32),
            half,
            half,
        ),
        in_specs=[smem(), vmem(), pl.BlockSpec(memory_space=pl.ANY)],
        out_specs=(vmem(), vmem(), vmem(), vmem()),
        scratch_shapes=[
            pltpu.VMEM((2 * ORDER, 2 * ORDER), BF16),
            pltpu.VMEM((2 * ORDER, 2 * ORDER), BF16),
            pltpu.VMEM((rows, ORDER), F32),
            pltpu.SemaphoreType.DMA,
        ],
        compiler_params=limit(ROTATION_LIMIT),
        name="rotation_turn",
    )(flag, gram_total, columns)


def turn(columns, turn_rows, early_is_back):
    half = jax.ShapeDtypeStruct((columns.shape[0] // 2, ORDER), F32)
    return pl.pallas_call(
        turn_kernel,
        out_shape=(half, half),
        in_specs=[smem(), vmem(), vmem()],
        out_specs=(vmem(), vmem()),
        scratch_shapes=[pltpu.VMEM((2 * ORDER, 2 * ORDER), BF16)] * 2,
        compiler_params=limit(16),
        cost_estimate=cost(12 * columns.shape[0] * ORDER * ORDER, 8 * columns.shape[0] * ORDER),
        name="turn",
    )(early_is_back, turn_rows, columns)


def turn_raw_kernel(rows_ref, x_ref, out_ref, high, low):
    rows = rows_ref[...]
    none = jnp.zeros_like(rows)
    upper = jnp.concatenate([rows, none], axis=0)
    lower = jnp.concatenate([none, rows], axis=0)
    store_weights(jnp.concatenate([upper, lower], axis=1).T, high, low)

    @pl.loop(0, out_ref.shape[0] // TILE, unroll=True)
    def _(tile):
        out_ref[tile_rows(tile, TILE)] = dot_three(packed(x_ref, tile), high, low)


def turn_raw(columns, half_rows):
    return pl.pallas_call(
        turn_raw_kernel,
        out_shape=jax.ShapeDtypeStruct((columns.shape[0] // 2, ORDER), F32),
        in_specs=[vmem(), vmem()],
        out_specs=vmem(),
        scratch_shapes=[pltpu.VMEM((2 * ORDER, ORDER), BF16)] * 2,
        compiler_params=limit(16),
        cost_estimate=cost(8 * columns.shape[0] * ORDER * ORDER, 6 * columns.shape[0] * ORDER),
        name="turn_raw",
    )(half_rows, columns)


def half_roll(value, axis):
    return pltpu.roll(value, HALF, axis)


def low_lanes(shape):
    return lax.broadcasted_iota(jnp.int32, shape, 1) < HALF


def pair_gram_kernel(core_ref, before_ref, own_ref, come_ref, out_ref, total):
    total[...] = jnp.zeros_like(total)

    @pl.loop(0, own_ref.shape[0] // TILE, unroll=True)
    def _(tile):
        rows = tile_rows(tile, TILE)
        high, low = split_two(jnp.concatenate([own_ref[rows], come_ref[rows]], axis=1))
        total[...] += dot_bf16(high, jnp.concatenate([high, low], axis=1), ((0,), (0,)))

    mixed = total[:, 2 * ORDER :]
    whole = total[:, : 2 * ORDER] + (mixed + mixed.T)
    tops = jnp.concatenate([whole[:HALF], whole[ORDER : ORDER + HALF]], axis=0)
    bottoms = jnp.concatenate([whole[HALF:ORDER], whole[ORDER + HALF :]], axis=0)
    first = low_lanes((ORDER, ORDER))
    gram = jnp.where(first, tops[:, :ORDER], half_roll(tops[:, ORDER:], 1)) + jnp.where(
        first, half_roll(bottoms[:, :ORDER], 1), bottoms[:, ORDER:]
    )
    swapped = half_roll(half_roll(gram, 1), 0)
    out_ref[...] = before_ref[...] + jnp.where(core_ref[0] == 1, swapped, gram)


def pair_gram(core, before, own, come):
    return pl.pallas_call(
        pair_gram_kernel,
        out_shape=jax.ShapeDtypeStruct((ORDER, ORDER), F32),
        in_specs=[smem(), vmem(), vmem(), vmem()],
        out_specs=vmem(),
        scratch_shapes=[pltpu.VMEM((2 * ORDER, 4 * ORDER), F32)],
        compiler_params=limit(16),
        cost_estimate=cost(16 * own.shape[0] * ORDER * ORDER, 8 * own.shape[0] * ORDER),
        name="pair_gram",
    )(core, before, own, come)


def finish_kernel(places, flags_ref, mine_ref, other_ref, *refs):
    parts, (out_ref, early_high, early_low, late_high, late_low, held, sems) = refs[:-7], refs[-7:]
    swap = flags_ref[1] == 1

    def ordered(rows):
        return jnp.where(swap, half_roll(half_roll(rows, 1), 0), rows)

    first = low_lanes((HALF, ORDER))
    late_rows = ordered(mine_ref[...])[:HALF]
    early_rows = ordered(other_ref[...])[HALF:]
    late_own, late_come = jnp.where(first, late_rows, 0.0), jnp.where(first, 0.0, late_rows)
    early_last, early_own = jnp.where(first, early_rows, 0.0), jnp.where(first, 0.0, early_rows)

    def store(upper, lower, lower_first, high, low):
        above = jnp.where(lower_first, lower, upper)
        below = jnp.where(lower_first, upper, lower)
        store_weights(jnp.concatenate([above, below], axis=0).T, high, low)

    is_back = flags_ref[0] == 1
    store(
        jnp.concatenate([half_roll(early_own, 1), early_last], axis=1),
        jnp.concatenate([early_own, half_roll(early_last, 1)], axis=1),
        is_back,
        early_high,
        early_low,
    )
    store(
        jnp.concatenate([late_own, half_roll(late_come, 1)], axis=1),
        jnp.concatenate([half_roll(late_own, 1), late_come], axis=1),
        jnp.logical_not(is_back),
        late_high,
        late_low,
    )
    late_lanes = low_lanes((TILE, ORDER)) == is_back

    def out_copy(tile):
        size = 2 * TILE
        return pltpu.make_async_copy(held.at[tile], out_ref.at[tile_rows(tile, size)], sems.at[tile])

    for index, (place, tiles) in enumerate(places):
        early_ref, late_ref, come_ref, last_ref = parts[4 * index : 4 * index + 4]

        @pl.loop(0, tiles, unroll=True)
        def _(tile):
            rows = tile_rows(tile, TILE)
            early = jnp.concatenate([early_ref[rows], last_ref[rows]], axis=1)
            late = jnp.concatenate([late_ref[rows], come_ref[rows]], axis=1)
            early = dot_three(early, early_high, early_low)
            late = dot_three(late, late_high, late_low)
            held[tile + place, :TILE] = jnp.where(late_lanes, late, early)
            held[tile + place, TILE:] = half_roll(jnp.where(late_lanes, early, late), 1)
            out_copy(tile + place).start()

    for tile in range(held.shape[0]):
        out_copy(tile).wait()


def finish(flags, mine, other, places, parts, rows):
    tiles = rows // (2 * TILE)
    return pl.pallas_call(
        functools.partial(finish_kernel, places),
        out_shape=jax.ShapeDtypeStruct((rows, ORDER), F32),
        in_specs=[smem()] + [vmem()] * (2 + len(parts)),
        out_specs=pl.BlockSpec(memory_space=pl.ANY),
        scratch_shapes=[
            pltpu.VMEM((2 * ORDER, ORDER), BF16),
            pltpu.VMEM((2 * ORDER, ORDER), BF16),
            pltpu.VMEM((2 * ORDER, ORDER), BF16),
            pltpu.VMEM((2 * ORDER, ORDER), BF16),
            pltpu.VMEM((tiles, 2 * TILE, ORDER), F32),
            pltpu.SemaphoreType.DMA((tiles,)),
        ],
        compiler_params=limit(24),
        name="finish",
    )(flags, mine, other, *parts)


def moved(array, target):
    rows, cols = lax.axis_size("row"), lax.axis_size("col")
    pairs = []
    for row in range(rows):
        for col in range(cols):
            to_row, to_col = target(row, col)
            pairs.append((row * cols + col, (to_row % rows) * cols + to_col % cols))
    return lax.ppermute(array, ("row", "col"), pairs)


def outward(row, col):
    return row, col + (1 if row % 2 == 0 else -1)


def inward(row, col):
    return row, col + (-1 if row % 2 == 0 else 1)


def inward_swapped(row, col):
    to_row, to_col = inward(row, col)
    return to_row ^ 1, to_col


def swap_rows(by):
    return lambda row, col: (row ^ by, col)


def summed(gram):
    for by in (2, 4, 14):
        gram = gram + moved(gram, swap_rows(by))
    return gram


def tied(first, *others):
    return lax.optimization_barrier((first, *others))[0]


def local(matrix, plan):
    rows = matrix.shape[0]
    tiles = rows // (2 * TILE)
    core = lax.axis_index("row") % 2
    leaver = plan[lax.axis_index("col")]
    early_is_back = leaver ^ core
    flag, core_flag = early_is_back.reshape(1), core.reshape(1)
    rest_tiles = tiles - RAW_TILES
    places = ((0, RAW_TILES), (RAW_TILES, rest_tiles))

    gram, sent = gram_and_raw(matrix)
    raw_come = moved(sent, outward)
    gram = gram + moved(gram, swap_rows(1))
    first_turn, half_turn, early_b, late_b = rotation_turn(flag, summed(gram), matrix)
    come_turn = moved(half_turn, inward_swapped)

    come_b = moved(early_b, outward)
    early_a, late_a = turn(sent, tied(first_turn, early_b, come_turn), flag)
    come_a = turn_raw(raw_come, come_turn)
    second = pair_gram(core_flag, jnp.zeros_like(gram), late_a, come_a)
    last_a = moved(tied(late_a, second, come_b), inward)
    last_b = moved(tied(late_b, second, come_b), inward)
    second = pair_gram(core_flag, second, late_b, come_b)
    second = second + moved(moved(second, swap_rows(1)), outward)
    mine = rotation_rows(summed(second))
    other = moved(mine, swap_rows(1))
    flags = jnp.stack([early_is_back, core])
    parts = [early_a, late_a, come_a, last_a, early_b, late_b, come_b, last_b]
    return finish(flags, mine, other, places, parts, rows)


def solution(mesh):
    in_specs = (P("row", "col"), P())
    out_specs = P("row", "col")
    return jax.shard_map(local, mesh=mesh, in_specs=in_specs, out_specs=out_specs, check_vma=False)
```
